256 devices in a mesh: row: 16 (over z_hi, y, core), col: 16 (over x, z_lo).
Axes of the slice: x: 4, y: 4, z: 8 (z_hi: 2, z_lo: 4; z = z_hi * 4 + z_lo), core: 2. Of those that a mesh axis runs over, the one named last changes fastest.
Arguments:
- tile_values: bfloat16 [90112, 128, 128], P(('row', 'col')), may hold values from 0.049804688 to 20
- tile_rows: int32 [90112], P(('row', 'col')), may hold values from 0 to 63
- tile_cols: int32 [90112], P(('row', 'col')), may hold values from 0 to 31
- seed_users: int32 [32, 16], replicated, may hold values from 0 to 131071
Outputs:
- hub: float32 [32, 131072], P(None, ('row', 'col'))
- authority: float32 [32, 65536], P(None, ('col', 'row'))
The draws below stay inside these ranges and needn't reach their ends.
All inputs are finite; a program needn't handle non-finite values.
Results may differ from the reference program's by a relative error of at most 0.0003.
Values may be sent and summed in bfloat16 or wider, within the bound.
No kernel may reach another device: no remote copies, remote signals or barrier semaphores. Data moves between devices by JAX's collectives and lax.ppermute only.
A program may use at most 64 MiB of HBM per device.

```python
import math
import jax
import jax.numpy as jnp
from jax import lax

SEEDS = 32
SEEDK = 16
ITERS = 2
TILES = 352
USERS = 131072
ITEMS = 65536
UB = 64
IB = 32
ALL_TILES = 90112
N_ROW = 16
N_COL = 16


def touch_ends(values, own_key, smallest, largest):
    index_at = [jax.random.randint(jax.random.fold_in(own_key, axis), (), 0, length) for axis, length in enumerate(values.shape)]
    main_axis = values.shape.index(max(values.shape))
    neighbour = index_at[:main_axis] + [(index_at[main_axis] + 1) % values.shape[main_axis]] + index_at[main_axis + 1:]
    return values.at[tuple(index_at)].set(smallest).at[tuple(neighbour)].set(largest)


def block_levels(stream_key, extent, cuts, low, high):
    def one(axis_at, parts):
        heights = jax.random.uniform(jax.random.fold_in(jax.random.fold_in(stream_key, 6), axis_at), (parts,), jnp.float32, low / len(cuts), high / len(cuts))
        return jnp.repeat(jnp.exp(heights), extent[axis_at] // parts).reshape((-1,) + (1,) * (len(extent) - axis_at - 1))

    factor_of = one(*cuts[0])
    for cut in cuts[1:]:
        factor_of = factor_of * one(*cut)
    return factor_of


def setup_inputs(seed: int = 0) -> dict:
    arg_keys = jax.random.split(jax.random.key(seed), 5)
    tile_values = jnp.clip(jnp.exp(math.log(20.0) - 5.9953784 * jax.random.uniform(arg_keys[0], (ALL_TILES, 128, 128), jnp.float32) ** block_levels(arg_keys[0], (ALL_TILES, 128, 128), ((0, 256),), -0.2, 0.2)), 0.049804688, 20.0).astype(jnp.bfloat16)
    tile_rows = touch_ends(jax.random.randint(arg_keys[1], (ALL_TILES,), 0, UB), jax.random.fold_in(arg_keys[1], 1), 0, UB - 1).astype(jnp.int32)
    tile_cols = touch_ends(jax.random.randint(arg_keys[2], (ALL_TILES,), 0, IB), jax.random.fold_in(arg_keys[2], 1), 0, IB - 1).astype(jnp.int32)
    seed_users = touch_ends(jax.random.randint(arg_keys[3], (SEEDS, SEEDK), 0, USERS), jax.random.fold_in(arg_keys[3], 1), 0, USERS - 1).astype(jnp.int32)
    return dict(tile_values=tile_values, tile_rows=tile_rows, tile_cols=tile_cols, seed_users=seed_users)


def reference(tile_values, tile_rows, tile_cols, seed_users):
    grid = N_ROW * N_COL
    values = tile_values.reshape(grid, TILES, 128, 128)
    rows = tile_rows.reshape(grid, TILES)
    cols = tile_cols.reshape(grid, TILES)
    cells = jnp.arange(grid, dtype=jnp.int32)
    user_ids = jnp.arange(USERS, dtype=jnp.int32)
    counts = lax.optimization_barrier(jnp.sum((seed_users[:, :, None] == user_ids[None, None, :]).astype(jnp.float32), axis=1))
    teleport = counts * jnp.float32((USERS / SEEDK) ** 0.5)

    def items_of(hub_wire):
        hub3 = hub_wire.reshape(SEEDS, USERS // 128, 128)

        def step(total, inputs):
            tile_v, tile_r, tile_c, cell = inputs
            grow = cell // N_COL * UB + tile_r
            gcol = cell % N_COL * IB + tile_c
            picked = hub3[:, grow, :].astype(jnp.float32)
            prod = jnp.einsum('stk,tkj->stj', picked, tile_v.astype(jnp.float32))
            return (total.at[:, gcol, :].add(prod), None)
        start = jnp.zeros((SEEDS, ITEMS // 128, 128), jnp.float32)
        total, _ = lax.scan(step, start, (values, rows, cols, cells))
        return total.reshape(SEEDS, ITEMS)

    def users_of(item_wire):
        item3 = item_wire.reshape(SEEDS, ITEMS // 128, 128)

        def step(total, inputs):
            tile_v, tile_r, tile_c, cell = inputs
            grow = cell // N_COL * UB + tile_r
            gcol = cell % N_COL * IB + tile_c
            picked = item3[:, gcol, :].astype(jnp.float32)
            prod = jnp.einsum('stj,tkj->stk', picked, tile_v.astype(jnp.float32))
            return (total.at[:, grow, :].add(prod), None)
        start = jnp.zeros((SEEDS, USERS // 128, 128), jnp.float32)
        total, _ = lax.scan(step, start, (values, rows, cols, cells))
        return total.reshape(SEEDS, USERS)
    hub = teleport
    authority = jnp.zeros((SEEDS, ITEMS), jnp.float32)
    for step_index in range(ITERS):
        item_raw = items_of(hub.astype(jnp.bfloat16))
        item_scale = lax.rsqrt(lax.optimization_barrier(jnp.sum(item_raw * item_raw, axis=1, keepdims=True)) / ITEMS + 1e-06)
        authority = item_raw * item_scale
        user_raw = users_of(authority.astype(jnp.bfloat16))
        user_scale = lax.rsqrt(lax.optimization_barrier(jnp.sum(user_raw * user_raw, axis=1, keepdims=True)) / USERS + 1e-06)
        hub = 0.85 * user_raw * user_scale + 0.15 * teleport
    return (hub, authority)
```

```python
import functools
import jax
import jax.numpy as jnp
import numpy as np
from jax import lax
from jax.experimental import pallas as pl
from jax.experimental.pallas import tpu as pltpu
from jax.sharding import PartitionSpec as P

SEEDK = 16
U_DEV = 512
I_DEV = 256
STEP = 32
SHRINK = 2.0**-16
GROW = 2.0**16


def teleport_tile(seed_ref, base, scale):
    seeds = seed_ref.shape[0]
    ids = base + lax.broadcasted_iota(jnp.int32, (seeds, 128), 1)
    count = jnp.zeros((seeds, 128), jnp.float32)
    for k in range(seed_ref.shape[1]):
        count += (seed_ref[:, k : k + 1] == ids).astype(jnp.float32)
    return count * scale


def teleport_kernel(base_ref, seed_ref, out_ref, *, scale):
    def body(t, carry):
        tile = teleport_tile(seed_ref, base_ref[0] + t * 128, scale)
        out_ref[t] = tile.astype(out_ref.dtype)
        return carry

    lax.fori_loop(0, out_ref.shape[0], body, 0)


def pass_kernel(src_ref, dst_ref, x_ref, w_ref, out_ref, acc_ref, *, contract, factor):
    step = pl.program_id(0)

    @pl.when(step == 0)
    def _():
        acc_ref[...] = jnp.zeros_like(acc_ref)

    for j in range(STEP):
        t = step * STEP + j
        prod = lax.dot_general(
            x_ref[src_ref[t]],
            w_ref[j],
            (((1,), (contract,)), ((), ())),
            preferred_element_type=jnp.float32,
        )
        acc_ref[dst_ref[t]] += prod

    @pl.when(step == pl.num_programs(0) - 1)
    def _():
        out_ref[...] = (acc_ref[...] * factor).astype(out_ref.dtype)


def tile_pass(src, dst, x, w, n_out, contract, factor, out_dtype):
    tiles = w.shape[0]
    seeds = x.shape[1]
    return pl.pallas_call(
        functools.partial(pass_kernel, contract=contract, factor=factor),
        grid_spec=pltpu.PrefetchScalarGridSpec(
            num_scalar_prefetch=2,
            grid=(tiles // STEP,),
            in_specs=[
                pl.BlockSpec(x.shape, lambda i, s, d: (0, 0, 0)),
                pl.BlockSpec((STEP, 128, 128), lambda i, s, d: (i, 0, 0)),
            ],
            out_specs=pl.BlockSpec((n_out, seeds, 128), lambda i, s, d: (0, 0, 0)),
            scratch_shapes=[pltpu.VMEM((n_out, seeds, 128), jnp.float32)],
        ),
        out_shape=jax.ShapeDtypeStruct((n_out, seeds, 128), out_dtype),
        compiler_params=pltpu.CompilerParams(vmem_limit_bytes=24 * 2**20),
    )(src, dst, x, w)


def reduce_shards(part, axis, n):
    tiles, seeds, edge = part.shape
    got = lax.all_to_all(part.reshape(n, tiles // n, seeds, edge), axis, 0, 0)
    return jnp.sum(got.astype(jnp.float32), axis=0)


def gather_shards(shard, axis, n):
    tiles, seeds, edge = shard.shape
    wire = jnp.broadcast_to(shard.astype(jnp.bfloat16)[None], (n, tiles, seeds, edge))
    return lax.all_to_all(wire, axis, 0, 0).reshape(n * tiles, seeds, edge)


def diag_mask(seeds, slot):
    lane = lax.broadcasted_iota(jnp.int32, (seeds, 128), 1)
    sub = lax.broadcasted_iota(jnp.int32, (seeds, 128), 0)
    return lane == sub + slot * seeds


def stat_kernel(x1_ref, y2_ref, got_ref, w2_ref, stat_ref):
    seeds = w2_ref.shape[1]
    w2_ref[...] = jnp.sum(got_ref[...], axis=0)

    def dot(a, b):
        return jnp.sum(jnp.sum(a * b, axis=0), axis=1, keepdims=True)

    x1, y2, w2 = x1_ref[...], y2_ref[...], w2_ref[...]
    spread = jnp.zeros((seeds, 128), jnp.float32)
    for slot, value in enumerate((dot(x1, x1), dot(x1, y2), dot(y2, y2), dot(w2, w2))):
        spread = jnp.where(diag_mask(seeds, slot), value, spread)
    stat_ref[...] = jnp.sum(spread, axis=0, keepdims=True)


def finish_kernel(
    base_ref, seed_ref, stat_ref, x1_ref, u1_ref, y2_ref, w2_ref, hub_ref, auth_ref, *, users, items, scale
):
    seeds = seed_ref.shape[0]

    def stat(slot):
        spread = jnp.where(diag_mask(seeds, slot), stat_ref[...], 0.0)
        return jnp.sum(spread, axis=1, keepdims=True)

    x1_sq, x1_y2, y2_sq, w2_sq = stat(0), stat(1), stat(2), stat(3)
    s_item1 = lax.rsqrt(x1_sq / items + 1e-06)
    gain = s_item1 * GROW
    s_user1 = lax.rsqrt(gain * gain * x1_y2 / users + 1e-06)
    alpha = 0.85 * s_item1 * s_user1 * (GROW * GROW)
    x2_sq = alpha * alpha * y2_sq + 0.3 * alpha * x1_y2 + 0.0225 * x1_sq
    s_item2 = lax.rsqrt(x2_sq / items + 1e-06)
    for t in range(auth_ref.shape[1] // 128):
        auth_ref[:, t * 128 : (t + 1) * 128] = (alpha * y2_ref[t] + 0.15 * x1_ref[t]) * s_item2
    raw_sq = alpha * alpha * w2_sq + 0.3 * alpha * y2_sq + 0.0225 * x1_y2
    out_gain = s_item2 * GROW
    s_user2 = lax.rsqrt(out_gain * out_gain * raw_sq / users + 1e-06)
    for t in range(hub_ref.shape[1] // 128):
        raw = (alpha * w2_ref[t] + 0.15 * u1_ref[t]) * out_gain
        tele = teleport_tile(seed_ref, base_ref[0] + t * 128, scale)
        hub_ref[:, t * 128 : (t + 1) * 128] = 0.85 * raw * s_user2 + 0.15 * tele


def per_device(tile_values, tile_rows, tile_cols, seed_users):
    n_rows = lax.axis_size("row")
    n_cols = lax.axis_size("col")
    row_index = lax.axis_index("row")
    cell = row_index * n_cols + lax.axis_index("col")
    seeds = seed_users.shape[0]
    edge = tile_values.shape[1]
    user_tiles = U_DEV * n_cols // edge
    item_tiles = I_DEV * n_rows // edge
    users = U_DEV * n_rows * n_cols
    items = I_DEV * n_rows * n_cols
    scale = float(np.float32((users / SEEDK) ** 0.5))
    smem = pl.BlockSpec(memory_space=pltpu.SMEM)
    vmem = pl.BlockSpec(memory_space=pltpu.VMEM)

    def to_items(hub, out_dtype, factor):
        return tile_pass(tile_rows, tile_cols, hub, tile_values, item_tiles, 0, factor, out_dtype)

    def to_users(item, out_dtype, factor):
        return tile_pass(tile_cols, tile_rows, item, tile_values, user_tiles, 1, factor, out_dtype)

    row_base = (row_index * (U_DEV * n_cols)).astype(jnp.int32).reshape(1)
    own_base = (cell * U_DEV).astype(jnp.int32).reshape(1)
    tele = pl.pallas_call(
        functools.partial(teleport_kernel, scale=scale),
        in_specs=[smem, vmem],
        out_specs=vmem,
        out_shape=jax.ShapeDtypeStruct((user_tiles, seeds, edge), jnp.bfloat16),
    )(row_base, seed_users)
    x1 = reduce_shards(to_items(tele, jnp.bfloat16, 1.0), "row", n_rows)
    u1 = reduce_shards(
        to_users(gather_shards(x1, "row", n_rows), jnp.bfloat16, SHRINK), "col", n_cols
    )
    y2 = reduce_shards(
        to_items(gather_shards(u1, "col", n_cols), jnp.float32, SHRINK), "row", n_rows
    )
    part = to_users(gather_shards(y2, "row", n_rows), jnp.float32, SHRINK)
    got = lax.all_to_all(part.reshape(n_cols, user_tiles // n_cols, seeds, edge), "col", 0, 0)
    w2, stat = pl.pallas_call(
        stat_kernel,
        in_specs=[vmem] * 3,
        out_specs=[vmem] * 2,
        out_shape=[
            jax.ShapeDtypeStruct((U_DEV // edge, seeds, edge), jnp.float32),
            jax.ShapeDtypeStruct((1, edge), jnp.float32),
        ],
    )(x1, y2, got)
    spread = jnp.broadcast_to(stat[None], (n_rows * n_cols, 1, edge))
    total = jnp.sum(lax.all_to_all(spread, ("row", "col"), 0, 0), axis=0)
    return pl.pallas_call(
        functools.partial(finish_kernel, users=users, items=items, scale=scale),
        in_specs=[smem] + [vmem] * 6,
        out_specs=[vmem] * 2,
        out_shape=[
            jax.ShapeDtypeStruct((seeds, U_DEV), jnp.float32),
            jax.ShapeDtypeStruct((seeds, I_DEV), jnp.float32),
        ],
    )(own_base, seed_users, total, x1, u1, y2, w2)


def solution(mesh):
    return jax.shard_map(
        per_device,
        mesh=mesh,
        in_specs=(P(("row", "col"), None, None), P(("row", "col")), P(("row", "col")), P()),
        out_specs=(P(None, ("row", "col")), P(None, ("col", "row"))),
        check_vma=False,
    )
```

```python
import functools
import jax
import jax.numpy as jnp
import numpy as np
from jax import lax
from jax.experimental import pallas as pl
from jax.experimental.pallas import tpu as pltpu
from jax.sharding import PartitionSpec as P

SEEDK = 16
U_DEV = 512
I_DEV = 256
EDGE = 128
UNROLL = 176
STREAM = 88
SHRINK = 2.0**-16
GROW = 2.0**16
MIB = 2**20
F32 = jnp.float32
BF16 = jnp.bfloat16
SMEM = pl.BlockSpec(memory_space=pltpu.SMEM)
VMEM = pl.BlockSpec(memory_space=pltpu.VMEM)

CORE, Y, ZHI = (0, 1), (1, 2), (3, 1)
ZLO, X = (0, 2), (2, 2)


def field(index, part):
    return (index >> part[0]) & ((1 << part[1]) - 1)


def shifted(x, axis, part, by):
    size = 1 << part[1]
    perm = []
    for i in range(16):
        old = field(i, part)
        perm.append((i, i + (((old + by) % size - old) << part[0])))
    return lax.ppermute(x, axis, perm)


def gathered(x, axis, part):
    size = 1 << part[1]
    return [x] + [shifted(x, axis, part, size - by) for by in range(1, size)]


def exchanged(chunks, axis, part):
    return [chunks[0]] + [shifted(c, axis, part, by) for by, c in enumerate(chunks) if by]


def added(parts):
    total = parts[0].astype(F32)
    for p in parts[1:]:
        total = total + p.astype(F32)
    return total


def seed_columns(seed_ref):
    k, seeds = seed_ref.shape
    diag = diag_mask(seeds, seeds, 0)
    rows = seed_ref[...].astype(F32)
    return [
        jnp.sum(jnp.where(diag, rows[i : i + 1], 0.0), axis=1, keepdims=True).astype(jnp.int32)
        for i in range(k)
    ]


def teleport_tile(columns, base, scale):
    seeds = columns[0].shape[0]
    ids = base + lax.broadcasted_iota(jnp.int32, (seeds, EDGE), 1)
    count = jnp.zeros((seeds, EDGE), F32)
    for column in columns:
        count = jnp.where(column == ids, count + 1.0, count)
    return count * scale


def multiply_tiles(src_ref, dst_ref, x_ref, w_ref, acc_ref, contract, first, count):
    for j in range(count):
        prod = lax.dot_general(
            x_ref[src_ref[first + j]],
            w_ref[j] if w_ref.shape[0] == count else w_ref[first + j],
            (((1,), (contract,)), ((), ())),
            preferred_element_type=F32,
        )
        acc_ref[dst_ref[first + j]] += prod


def store_chunks(acc_ref, out_refs, factor):
    start = 0
    for out in out_refs:
        rows = out.shape[0]
        out[...] = (acc_ref[start : start + rows] * factor).astype(out.dtype)
        start += rows


def first_kernel(src_ref, dst_ref, base_ref, seed_ref, w_ref, *rest, scale):
    *out_refs, x_ref, wide_ref, acc_ref = rest
    step = pl.program_id(0)

    @pl.when(step == 0)
    def _():
        acc_ref[...] = jnp.zeros_like(acc_ref)
        for k, column in enumerate(seed_columns(seed_ref)):
            wide_ref[k] = jnp.broadcast_to(column - base_ref[0], wide_ref.shape[1:])

        def body(t, carry):
            ids = t * EDGE + lax.broadcasted_iota(jnp.int32, wide_ref.shape[1:], 1)
            count = jnp.zeros(wide_ref.shape[1:], F32)
            for k in range(wide_ref.shape[0]):
                count = jnp.where(wide_ref[k] == ids, count + 1.0, count)
            x_ref[t] = (count * scale).astype(x_ref.dtype)
            return carry

        lax.fori_loop(0, x_ref.shape[0], body, 0)

    multiply_tiles(src_ref, dst_ref, x_ref, w_ref, acc_ref, 0, step * STREAM, STREAM)

    @pl.when(step == pl.num_programs(0) - 1)
    def _():
        store_chunks(acc_ref, out_refs, 1.0)


def first_pass(src, dst, base, seed_t, w, n_src, outs, scale):
    seeds = seed_t.shape[1]
    n_dst = sum(rows for rows, _ in outs)
    return pl.pallas_call(
        functools.partial(first_kernel, scale=scale),
        grid_spec=pltpu.PrefetchScalarGridSpec(
            num_scalar_prefetch=3,
            grid=(w.shape[0] // STREAM,),
            in_specs=[
                pl.BlockSpec(seed_t.shape, lambda i, *_: (0, 0)),
                pl.BlockSpec((STREAM, EDGE, EDGE), lambda i, *_: (i, 0, 0)),
            ],
            out_specs=[pl.BlockSpec((rows, seeds, EDGE), lambda i, *_: (0, 0, 0)) for rows, _ in outs],
            scratch_shapes=[
                pltpu.VMEM((n_src, seeds, EDGE), BF16),
                pltpu.VMEM((seed_t.shape[0], seeds, EDGE), jnp.int32),
                pltpu.VMEM((n_dst, seeds, EDGE), F32),
            ],
        ),
        out_shape=[jax.ShapeDtypeStruct((rows, seeds, EDGE), dtype) for rows, dtype in outs],
        compiler_params=pltpu.CompilerParams(vmem_limit_bytes=56 * MIB),
    )(src, dst, base, seed_t, w)


def pass_kernel(src_ref, dst_ref, w_ref, *rest, contract, n_in):
    in_refs, (*out_refs, x_ref, acc_ref) = rest[:n_in], rest[n_in:]
    acc_ref[...] = jnp.zeros_like(acc_ref)
    start = 0
    for ref in in_refs:
        x_ref[start : start + ref.shape[0]] = ref[...]
        start += ref.shape[0]

    def body(i, carry):
        multiply_tiles(src_ref, dst_ref, x_ref, w_ref, acc_ref, contract, i * UNROLL, UNROLL)
        return carry

    lax.fori_loop(0, w_ref.shape[0] // UNROLL, body, 0)
    store_chunks(acc_ref, out_refs, SHRINK)


def tile_pass(src, dst, w, parts, contract, outs):
    seeds = parts[0].shape[1]
    n_src = sum(p.shape[0] for p in parts)
    n_dst = sum(rows for rows, _ in outs)
    return pl.pallas_call(
        functools.partial(pass_kernel, contract=contract, n_in=len(parts)),
        in_specs=[SMEM] * 2 + [VMEM] * (1 + len(parts)),
        out_specs=[VMEM] * len(outs),
        scratch_shapes=[
            pltpu.VMEM((n_src, seeds, EDGE), BF16),
            pltpu.VMEM((n_dst, seeds, EDGE), F32),
        ],
        out_shape=[jax.ShapeDtypeStruct((rows, seeds, EDGE), dtype) for rows, dtype in outs],
        compiler_params=pltpu.CompilerParams(vmem_limit_bytes=20 * MIB),
    )(src, dst, w, *parts)


def diag_mask(seeds, width, slot):
    lane = lax.broadcasted_iota(jnp.int32, (seeds, width), 1)
    sub = lax.broadcasted_iota(jnp.int32, (seeds, width), 0)
    return lane == sub + slot * seeds


def stat_kernel(x1_ref, y2_ref, *rest):
    *got_refs, w2_ref, stat_ref = rest
    seeds = w2_ref.shape[1]
    w2_ref[...] = added([ref[...] for ref in got_refs])

    def dot(a, b):
        return jnp.sum(jnp.sum(a * b, axis=0), axis=1, keepdims=True)

    x1, y2, w2 = x1_ref[...], y2_ref[...], w2_ref[...]
    spread = jnp.zeros((seeds, EDGE), F32)
    for slot, value in enumerate((dot(x1, x1), dot(x1, y2), dot(y2, y2), dot(w2, w2))):
        spread = jnp.where(diag_mask(seeds, EDGE, slot), value, spread)
    stat_ref[...] = jnp.broadcast_to(jnp.sum(spread, axis=0, keepdims=True), stat_ref.shape)


def finish_kernel(
    base_ref, seed_ref, stat_ref, x1_ref, u1_ref, y2_ref, w2_ref, hub_ref, auth_ref, *, users, items, scale
):
    seeds = seed_ref.shape[1]
    total = jnp.sum(stat_ref[...], axis=0, keepdims=True)

    def stat(slot):
        return jnp.sum(jnp.where(diag_mask(seeds, EDGE, slot), total, 0.0), axis=1, keepdims=True)

    x1_sq, x1_y2, y2_sq, w2_sq = stat(0), stat(1), stat(2), stat(3)
    s_item1 = lax.rsqrt(x1_sq / items + 1e-06)
    gain = s_item1 * GROW
    s_user1 = lax.rsqrt(gain * gain * x1_y2 / users + 1e-06)
    alpha = 0.85 * s_item1 * s_user1 * (GROW * GROW)
    x2_sq = alpha * alpha * y2_sq + 0.3 * alpha * x1_y2 + 0.0225 * x1_sq
    s_item2 = lax.rsqrt(x2_sq / items + 1e-06)
    for t in range(auth_ref.shape[1] // EDGE):
        auth_ref[:, t * EDGE : (t + 1) * EDGE] = (alpha * y2_ref[t] + 0.15 * x1_ref[t]) * s_item2
    raw_sq = alpha * alpha * w2_sq + 0.3 * alpha * y2_sq + 0.0225 * x1_y2
    out_gain = s_item2 * GROW
    s_user2 = lax.rsqrt(out_gain * out_gain * raw_sq / users + 1e-06)
    columns = seed_columns(seed_ref)
    for t in range(hub_ref.shape[1] // EDGE):
        raw = (alpha * w2_ref[t] + 0.15 * u1_ref[t]) * out_gain
        tele = teleport_tile(columns, base_ref[0] + t * EDGE, scale)
        hub_ref[:, t * EDGE : (t + 1) * EDGE] = 0.85 * raw * s_user2 + 0.15 * tele


def per_device(tile_values, tile_rows, tile_cols, seed_users):
    n_rows = lax.axis_size("row")
    n_cols = lax.axis_size("col")
    row = lax.axis_index("row").astype(jnp.int32)
    col = lax.axis_index("col").astype(jnp.int32)
    seeds = seed_users.shape[0]
    users = U_DEV * n_rows * n_cols
    items = I_DEV * n_rows * n_cols
    scale = float(np.float32((users / SEEDK) ** 0.5))
    seed_t = seed_users.T
    row_base = (row * (U_DEV * n_cols)).reshape(1)
    own_base = ((row * n_cols + col) * U_DEV).reshape(1)
    core, y, zhi = field(row, CORE), field(row, Y), field(row, ZHI)
    zlo, x = field(col, ZLO), field(col, X)

    t_half = (((tile_cols >> 1) & 1) ^ core) * 16
    t_zhi, t_y, t_q = tile_cols >> 4, (tile_cols >> 2) & 3, tile_cols & 1
    item_whole = t_half + t_zhi * 8 + t_y * 2 + t_q
    item_by_y = t_half + ((t_y - y) & 3) * 4 + t_zhi * 2 + t_q
    t_x = ((tile_rows >> 4) - x) & 3
    user_whole = t_x * 16 + (tile_rows & 15)
    user_by_z = t_x * 16 + ((((tile_rows >> 2) & 3) - zlo) & 3) * 4 + (tile_rows & 3)

    keep, send = first_pass(
        tile_rows, item_whole, row_base, seed_t, tile_values, 64, [(16, BF16)] * 2, scale
    )
    part = added(exchanged([keep, send], "row", CORE)).astype(BF16)
    part = added(gathered(part, "row", ZHI)).astype(BF16)
    x1_all = added(gathered(part, "row", Y))
    x1 = lax.dynamic_slice_in_dim(x1_all, (zhi * 4 + y) * 2, 2, 0)

    chunks = tile_pass(
        item_whole, user_whole, tile_values, gathered(x1_all.astype(BF16), "row", CORE), 1, [(16, BF16)] * 4
    )
    part = added(exchanged(chunks, "col", X)).astype(BF16)
    for bit in (1, 0):
        part = added(gathered(part, "col", (bit, 1)))
        u1 = lax.dynamic_slice_in_dim(part, zlo * 4, 4, 0)
        part = part.astype(BF16)

    chunks = tile_pass(
        user_whole, item_by_y, tile_values, gathered(part, "col", X), 0, [(16, F32)] * 2
    )
    part = added(exchanged(chunks, "row", CORE))
    part = added(exchanged([part[i * 4 : i * 4 + 4] for i in range(4)], "row", Y))
    part = added(gathered(part, "row", ZHI))
    y2 = lax.dynamic_slice_in_dim(part, zhi * 2, 2, 0)
    half = jnp.concatenate(gathered(part.astype(BF16), "row", Y), axis=0)

    chunks = tile_pass(
        item_by_y, user_by_z, tile_values, gathered(half, "row", CORE), 1, [(16, F32)] * 4
    )
    part = added(exchanged(chunks, "col", X))
    got = exchanged([part[i * 4 : i * 4 + 4] for i in range(4)], "col", ZLO)
    small = pltpu.CompilerParams(vmem_limit_bytes=8 * MIB)
    w2, stat = pl.pallas_call(
        stat_kernel,
        in_specs=[VMEM] * (2 + len(got)),
        out_specs=[VMEM] * 2,
        out_shape=[
            jax.ShapeDtypeStruct((U_DEV // EDGE, seeds, EDGE), F32),
            jax.ShapeDtypeStruct((n_rows * n_cols, EDGE), F32),
        ],
        compiler_params=small,
    )(x1, y2, *got)
    stats = lax.all_to_all(stat.reshape(n_rows * n_cols, 1, EDGE), ("row", "col"), 0, 0)
    return pl.pallas_call(
        functools.partial(finish_kernel, users=users, items=items, scale=scale),
        in_specs=[SMEM] + [VMEM] * 6,
        out_specs=[VMEM] * 2,
        out_shape=[
            jax.ShapeDtypeStruct((seeds, U_DEV), F32),
            jax.ShapeDtypeStruct((seeds, I_DEV), F32),
        ],
        compiler_params=small,
    )(own_base, seed_t, stats.reshape(n_rows * n_cols, EDGE), x1, u1, y2, w2)


def solution(mesh):
    return jax.shard_map(
        per_device,
        mesh=mesh,
        in_specs=(P(("row", "col"), None, None), P(("row", "col")), P(("row", "col")), P()),
        out_specs=(P(None, ("row", "col")), P(None, ("col", "row"))),
        check_vma=False,
    )
```

```python
import functools
import jax
import jax.numpy as jnp
import numpy as np
from jax import lax
from jax.experimental import pallas as pl
from jax.experimental.pallas import tpu as pltpu
from jax.sharding import PartitionSpec as P

SEEDK = 16
U_DEV = 512
I_DEV = 256
EDGE = 128
UNROLL = 176
STREAM = 88
SHRINK = 2.0**-16
GROW = 2.0**16
MIB = 2**20
F32 = jnp.float32
BF16 = jnp.bfloat16
SMEM = pl.BlockSpec(memory_space=pltpu.SMEM)
VMEM = pl.BlockSpec(memory_space=pltpu.VMEM)

CORE, Y, ZHI = (0, 1), (1, 2), (3, 1)
ZLO, X = (0, 2), (2, 2)


def field(index, part):
    return (index >> part[0]) & ((1 << part[1]) - 1)


def swapped(x, axis, part, by):
    return lax.ppermute(x, axis, [(i, i ^ (by << part[0])) for i in range(16)])


def gathered(x, axis, part):
    return [x] + [swapped(x, axis, part, by) for by in range(1, 1 << part[1])]


def exchanged(chunks, axis, part):
    return [chunks[0]] + [swapped(c, axis, part, by) for by, c in enumerate(chunks) if by]


def added(parts):
    total = parts[0].astype(F32)
    for p in parts[1:]:
        total = total + p.astype(F32)
    return total


def add_kernel(held_ref, *refs, n_in):
    total = added([ref[...] for ref in refs[:n_in]])
    for out in refs[n_in:]:
        out[...] = total.astype(out.dtype)


def add_parts(held, parts, dtypes):
    return pl.pallas_call(
        functools.partial(add_kernel, n_in=len(parts)),
        in_specs=[VMEM] * (1 + len(parts)),
        out_specs=[VMEM] * len(dtypes),
        out_shape=[jax.ShapeDtypeStruct(parts[0].shape, dtype) for dtype in dtypes],
        compiler_params=pltpu.CompilerParams(vmem_limit_bytes=8 * MIB),
    )(held, *parts)


def seed_columns(seed_ref):
    k, seeds = seed_ref.shape
    diag = diag_mask(seeds, seeds, 0)
    rows = seed_ref[...].astype(F32)
    return [
        jnp.sum(jnp.where(diag, rows[i : i + 1], 0.0), axis=1, keepdims=True).astype(jnp.int32)
        for i in range(k)
    ]


def teleport_tile(columns, base, scale):
    seeds = columns[0].shape[0]
    ids = base + lax.broadcasted_iota(jnp.int32, (seeds, EDGE), 1)
    count = jnp.zeros((seeds, EDGE), F32)
    for column in columns:
        count = jnp.where(column == ids, count + 1.0, count)
    return count * scale


def multiply_tiles(src_ref, dst_ref, x_ref, w_ref, acc_ref, contract, first, count):
    for j in range(count):
        prod = lax.dot_general(
            x_ref[src_ref[first + j]],
            w_ref[first + j],
            (((1,), (contract,)), ((), ())),
            preferred_element_type=F32,
        )
        acc_ref[dst_ref[first + j]] += prod


def store_chunks(acc_ref, out_refs, factor):
    start = 0
    for out in out_refs:
        rows = out.shape[0]
        out[...] = (acc_ref[start : start + rows] * factor).astype(out.dtype)
        start += rows


def first_kernel(src_ref, dst_ref, base_ref, seed_ref, w_ref, held_ref, *rest, scale):
    *out_refs, x_ref, wide_ref, acc_ref, sem = rest
    copies = []
    for i in range(held_ref.shape[0] // STREAM):
        part = pl.ds(i * STREAM, STREAM)
        copies.append(pltpu.make_async_copy(w_ref.at[part], held_ref.at[part], sem.at[i]))
        copies[-1].start()
    acc_ref[...] = jnp.zeros_like(acc_ref)
    last = x_ref.shape[0] * EDGE
    for k, column in enumerate(seed_columns(seed_ref)):
        local = column - base_ref[0]
        local = jnp.where((local >= 0) & (local < last), local, -1)
        wide_ref[k] = jnp.broadcast_to(local, wide_ref.shape[1:]).astype(wide_ref.dtype)

    lanes = lax.broadcasted_iota(jnp.int32, wide_ref.shape[1:], 1)

    def body(t, carry):
        ids = (t * EDGE + lanes).astype(wide_ref.dtype)
        count = jnp.zeros(ids.shape, ids.dtype)
        one = jnp.ones(ids.shape, ids.dtype)
        for k in range(wide_ref.shape[0]):
            count = count + jnp.where(wide_ref[k] == ids, one, jnp.zeros_like(one))
        x_ref[t ^ base_ref[1]] = (count.astype(F32) * scale).astype(x_ref.dtype)
        return carry

    lax.fori_loop(0, x_ref.shape[0], body, 0, unroll=4)
    for i, copy in enumerate(copies):
        copy.wait()
        multiply_tiles(src_ref, dst_ref, x_ref, held_ref, acc_ref, 0, i * STREAM, STREAM)
    store_chunks(acc_ref, out_refs, 1.0)


def first_pass(src, dst, base, seed_t, w, n_src, outs, scale):
    seeds = seed_t.shape[1]
    n_dst = sum(rows for rows, _ in outs)
    return pl.pallas_call(
        functools.partial(first_kernel, scale=scale),
        in_specs=[SMEM] * 3 + [VMEM, pl.BlockSpec(memory_space=pltpu.HBM)],
        out_specs=[VMEM] * (1 + len(outs)),
        scratch_shapes=[
            pltpu.VMEM((n_src, seeds, EDGE), BF16),
            pltpu.VMEM((seed_t.shape[0], seeds, EDGE), jnp.int16),
            pltpu.VMEM((n_dst, seeds, EDGE), F32),
            pltpu.SemaphoreType.DMA((w.shape[0] // STREAM,)),
        ],
        out_shape=[pltpu.VMEM(w.shape, w.dtype)]
        + [jax.ShapeDtypeStruct((rows, seeds, EDGE), dtype) for rows, dtype in outs],
        compiler_params=pltpu.CompilerParams(vmem_limit_bytes=49 * MIB),
    )(src, dst, base, seed_t, w)


def pass_kernel(src_ref, dst_ref, w_ref, *rest, contract, n_in):
    in_refs, (*out_refs, x_ref, acc_ref) = rest[:n_in], rest[n_in:]
    acc_ref[...] = jnp.zeros_like(acc_ref)
    start = 0
    for ref in in_refs:
        x_ref[start : start + ref.shape[0]] = ref[...]
        start += ref.shape[0]

    def body(i, carry):
        multiply_tiles(src_ref, dst_ref, x_ref, w_ref, acc_ref, contract, i * UNROLL, UNROLL)
        return carry

    lax.fori_loop(0, w_ref.shape[0] // UNROLL, body, 0)
    store_chunks(acc_ref, out_refs, SHRINK)


def tile_pass(src, dst, w, parts, contract, outs):
    seeds = parts[0].shape[1]
    n_src = sum(p.shape[0] for p in parts)
    n_dst = sum(rows for rows, _ in outs)
    return pl.pallas_call(
        functools.partial(pass_kernel, contract=contract, n_in=len(parts)),
        in_specs=[SMEM] * 2 + [VMEM] * (1 + len(parts)),
        out_specs=[VMEM] * len(outs),
        scratch_shapes=[
            pltpu.VMEM((n_src, seeds, EDGE), BF16),
            pltpu.VMEM((n_dst, seeds, EDGE), F32),
        ],
        out_shape=[jax.ShapeDtypeStruct((rows, seeds, EDGE), dtype) for rows, dtype in outs],
        compiler_params=pltpu.CompilerParams(vmem_limit_bytes=20 * MIB),
    )(src, dst, w, *parts)


def diag_mask(seeds, width, slot):
    lane = lax.broadcasted_iota(jnp.int32, (seeds, width), 1)
    sub = lax.broadcasted_iota(jnp.int32, (seeds, width), 0)
    return lane == sub + slot * seeds


def stat_kernel(x1_ref, y2_ref, *rest):
    *got_refs, w2_ref, stat_ref = rest
    seeds = w2_ref.shape[1]
    w2_ref[...] = added([ref[...] for ref in got_refs])

    def dot(a, b):
        return jnp.sum(jnp.sum(a * b, axis=0), axis=1, keepdims=True)

    x1, y2, w2 = x1_ref[...], y2_ref[...], w2_ref[...]
    spread = jnp.zeros((seeds, EDGE), F32)
    for slot, value in enumerate((dot(x1, x1), dot(x1, y2), dot(y2, y2), dot(w2, w2))):
        spread = jnp.where(diag_mask(seeds, EDGE, slot), value, spread)
    stat_ref[...] = jnp.broadcast_to(jnp.sum(spread, axis=0, keepdims=True), stat_ref.shape)


def finish_kernel(
    base_ref, seed_ref, stat_ref, x1_ref, u1_ref, y2_ref, w2_ref, hub_ref, auth_ref, *, users, items, scale
):
    seeds = seed_ref.shape[1]
    total = jnp.sum(stat_ref[...], axis=0, keepdims=True)

    def stat(slot):
        return jnp.sum(jnp.where(diag_mask(seeds, EDGE, slot), total, 0.0), axis=1, keepdims=True)

    x1_sq, x1_y2, y2_sq, w2_sq = stat(0), stat(1), stat(2), stat(3)
    s_item1 = lax.rsqrt(x1_sq / items + 1e-06)
    gain = s_item1 * GROW
    s_user1 = lax.rsqrt(gain * gain * x1_y2 / users + 1e-06)
    alpha = 0.85 * s_item1 * s_user1 * (GROW * GROW)
    x2_sq = alpha * alpha * y2_sq + 0.3 * alpha * x1_y2 + 0.0225 * x1_sq
    s_item2 = lax.rsqrt(x2_sq / items + 1e-06)
    for t in range(auth_ref.shape[1] // EDGE):
        auth_ref[:, t * EDGE : (t + 1) * EDGE] = (alpha * y2_ref[t] + 0.15 * x1_ref[t]) * s_item2
    raw_sq = alpha * alpha * w2_sq + 0.3 * alpha * y2_sq + 0.0225 * x1_y2
    out_gain = s_item2 * GROW
    s_user2 = lax.rsqrt(out_gain * out_gain * raw_sq / users + 1e-06)
    columns = seed_columns(seed_ref)
    for t in range(hub_ref.shape[1] // EDGE):
        raw = (alpha * w2_ref[t] + 0.15 * u1_ref[t]) * out_gain
        tele = teleport_tile(columns, base_ref[0] + t * EDGE, scale)
        hub_ref[:, t * EDGE : (t + 1) * EDGE] = 0.85 * raw * s_user2 + 0.15 * tele


def per_device(tile_values, tile_rows, tile_cols, seed_users):
    n_rows = lax.axis_size("row")
    n_cols = lax.axis_size("col")
    row = lax.axis_index("row").astype(jnp.int32)
    col = lax.axis_index("col").astype(jnp.int32)
    seeds = seed_users.shape[0]
    users = U_DEV * n_rows * n_cols
    items = I_DEV * n_rows * n_cols
    scale = float(np.float32((users / SEEDK) ** 0.5))
    seed_t = seed_users.T
    row_base = jnp.stack([row * (U_DEV * n_cols), field(col, X) * 16])
    own_base = ((row * n_cols + col) * U_DEV).reshape(1)
    core, y, zhi = field(row, CORE), field(row, Y), field(row, ZHI)
    zlo, x = field(col, ZLO), field(col, X)

    t_half = (((tile_cols >> 1) & 1) ^ core) * 16
    t_zhi, t_y, t_q = tile_cols >> 4, (tile_cols >> 2) & 3, tile_cols & 1
    item_whole = t_half + t_zhi * 8 + t_y * 2 + t_q
    item_by_y = t_half + (t_y ^ y) * 4 + t_zhi * 2 + t_q
    t_x = (tile_rows >> 4) ^ x
    user_whole = t_x * 16 + (tile_rows & 15)
    user_by_z = t_x * 16 + (((tile_rows >> 2) & 3) ^ zlo) * 4 + (tile_rows & 3)

    held, keep, send = first_pass(
        user_whole, item_whole, row_base, seed_t, tile_values, 64, [(16, BF16)] * 2, scale
    )
    (part,) = add_parts(held, exchanged([keep, send], "row", CORE), [BF16])
    (part,) = add_parts(held, gathered(part, "row", ZHI), [BF16])
    x1_all, part = add_parts(held, gathered(part, "row", Y), [F32, BF16])
    x1 = lax.dynamic_slice_in_dim(x1_all, (zhi * 4 + y) * 2, 2, 0)

    chunks = tile_pass(
        item_whole, user_whole, held, gathered(part, "row", CORE), 1, [(16, BF16)] * 4
    )
    (part,) = add_parts(held, exchanged(chunks, "col", X), [BF16])
    (part,) = add_parts(held, gathered(part, "col", (1, 1)), [BF16])
    u1_all, part = add_parts(held, gathered(part, "col", (0, 1)), [F32, BF16])
    u1 = lax.dynamic_slice_in_dim(u1_all, zlo * 4, 4, 0)

    chunks = tile_pass(
        user_whole, item_by_y, held, gathered(part, "col", X), 0, [(16, F32)] * 2
    )
    (part,) = add_parts(held, exchanged(chunks, "row", CORE), [F32])
    (part,) = add_parts(held, exchanged([part[i * 4 : i * 4 + 4] for i in range(4)], "row", Y), [F32])
    y2_all, part = add_parts(held, gathered(part, "row", ZHI), [F32, BF16])
    y2 = lax.dynamic_slice_in_dim(y2_all, zhi * 2, 2, 0)
    half = jnp.concatenate(gathered(part, "row", Y), axis=0)

    chunks = tile_pass(
        item_by_y, user_by_z, held, gathered(half, "row", CORE), 1, [(16, F32)] * 4
    )
    part = added(exchanged(chunks, "col", X))
    got = exchanged([part[i * 4 : i * 4 + 4] for i in range(4)], "col", ZLO)
    small = pltpu.CompilerParams(vmem_limit_bytes=8 * MIB)
    w2, stat = pl.pallas_call(
        stat_kernel,
        in_specs=[VMEM] * (2 + len(got)),
        out_specs=[VMEM] * 2,
        out_shape=[
            jax.ShapeDtypeStruct((U_DEV // EDGE, seeds, EDGE), F32),
            jax.ShapeDtypeStruct((n_rows * n_cols, EDGE), F32),
        ],
        compiler_params=small,
    )(x1, y2, *got)
    stats = lax.all_to_all(stat.reshape(n_rows * n_cols, 1, EDGE), ("row", "col"), 0, 0)
    return pl.pallas_call(
        functools.partial(finish_kernel, users=users, items=items, scale=scale),
        in_specs=[SMEM] + [VMEM] * 6,
        out_specs=[VMEM] * 2,
        out_shape=[
            jax.ShapeDtypeStruct((seeds, U_DEV), F32),
            jax.ShapeDtypeStruct((seeds, I_DEV), F32),
        ],
        compiler_params=small,
    )(own_base, seed_t, stats.reshape(n_rows * n_cols, EDGE), x1, u1, y2, w2)


def solution(mesh):
    return jax.shard_map(
        per_device,
        mesh=mesh,
        in_specs=(P(("row", "col"), None, None), P(("row", "col")), P(("row", "col")), P()),
        out_specs=(P(None, ("row", "col")), P(None, ("col", "row"))),
        check_vma=False,
    )
```

```python
import functools
import jax
import jax.numpy as jnp
import numpy as np
from jax import lax
from jax.experimental import pallas as pl
from jax.experimental.pallas import tpu as pltpu
from jax.sharding import PartitionSpec as P

SEEDK = 16
U_DEV = 512
I_DEV = 256
EDGE = 128
UNROLL = 176
STREAM = 88
SHRINK = 2.0**-16
GROW = 2.0**16
MIB = 2**20
LIGHT = pl.CostEstimate(flops=10**6, bytes_accessed=10**5, transcendentals=0)
F32 = jnp.float32
BF16 = jnp.bfloat16
F16 = jnp.float16
WIRE = F32
SMEM = pl.BlockSpec(memory_space=pltpu.SMEM)
VMEM = pl.BlockSpec(memory_space=pltpu.VMEM)

CORE, Y, ZHI = (0, 1), (1, 2), (3, 1)
ZLO, X = (0, 2), (2, 2)


HALVES_ZY = [[z * 16 + y * 4 + h * 2 + q for z in range(2) for y in range(4) for q in range(2)] for h in range(2)]
HALVES_YZ = [[z * 16 + y * 4 + h * 2 + q for y in range(4) for z in range(2) for q in range(2)] for h in range(2)]
QUARTERS = [list(range(c * 16, c * 16 + 16)) for c in range(4)]


def field(index, part):
    return (index >> part[0]) & ((1 << part[1]) - 1)


def swapped(x, axis, part, by):
    return lax.ppermute(x, axis, [(i, i ^ (by << part[0])) for i in range(16)])


def gathered(x, axis, part):
    return [x] + [swapped(x, axis, part, by) for by in range(1, 1 << part[1])]


def exchanged(chunks, axis, part):
    return [chunks[0]] + [swapped(c, axis, part, by) for by, c in enumerate(chunks) if by]


def added(parts):
    total = parts[0].astype(F32)
    for p in parts[1:]:
        total = total + p.astype(F32)
    return total


def add_kernel(*refs, n_in):
    total = added([ref[...] for ref in refs[1 : 1 + n_in]])
    for out in refs[1 + n_in :]:
        out[...] = total.astype(out.dtype)


def add_parts(held, parts, dtypes):
    return pl.pallas_call(
        functools.partial(add_kernel, n_in=len(parts)),
        in_specs=[VMEM] * (1 + len(parts)),
        out_specs=[VMEM] * len(dtypes),
        out_shape=[jax.ShapeDtypeStruct(parts[0].shape, dtype) for dtype in dtypes],
        compiler_params=pltpu.CompilerParams(vmem_limit_bytes=8 * MIB),
        cost_estimate=LIGHT,
    )(held, *parts)


def add_scaled(own, others):
    total = own
    for other in others:
        wide = other.astype(F32)
        total = total + wide[:-1] * jnp.exp2(wide[-1:])
    return total


def seed_columns(seed_ref):
    k, seeds = seed_ref.shape
    diag = diag_mask(seeds, seeds, 0)
    rows = seed_ref[...].astype(F32)
    return [
        jnp.sum(jnp.where(diag, rows[i : i + 1], 0.0), axis=1, keepdims=True).astype(jnp.int32)
        for i in range(k)
    ]


def teleport_tile(columns, base, scale):
    seeds = columns[0].shape[0]
    ids = base + lax.broadcasted_iota(jnp.int32, (seeds, EDGE), 1)
    count = jnp.zeros((seeds, EDGE), F32)
    for column in columns:
        count = jnp.where(column == ids, count + 1.0, count)
    return count * scale


def multiply_tiles(src_ref, dst_ref, masks, x_ref, w_ref, acc_ref, first, count, base, flip=0):
    for j in range(count):
        tile = w_ref[base + first + j]
        prod = lax.dot_general(
            x_ref[src_ref[first + j]],
            tile,
            (((1,), (0,)), ((), ())),
            preferred_element_type=F32,
        )
        acc_ref[dst_ref[first + j]] += prod
        if flip:
            w_ref[flip + first + j] = tile.T


def store_chunks(acc_ref, out_refs, orders, factor):
    for out, order in zip(out_refs, orders):
        for i, tile in enumerate(order):
            out[i] = (acc_ref[tile] * factor).astype(out.dtype)


def first_kernel(src_ref, dst_ref, plan_ref, seed_ref, w_ref, held_ref, *rest, orders, scale):
    *out_refs, x_ref, wide_ref, acc_ref, sem = rest
    copies = []
    tiles = w_ref.shape[0]
    for i in range(tiles // STREAM):
        part = pl.ds(i * STREAM, STREAM)
        copies.append(pltpu.make_async_copy(w_ref.at[part], held_ref.at[part], sem.at[i]))
        copies[-1].start()
    acc_ref[...] = jnp.zeros_like(acc_ref)
    last = x_ref.shape[0] * EDGE
    for k, column in enumerate(seed_columns(seed_ref)):
        local = column - plan_ref[2]
        local = jnp.where((local >= 0) & (local < last), local, -1)
        wide_ref[k] = jnp.broadcast_to(local, wide_ref.shape[1:]).astype(wide_ref.dtype)

    lanes = lax.broadcasted_iota(jnp.int32, wide_ref.shape[1:], 1)

    def body(t, carry):
        ids = (t * EDGE + lanes).astype(wide_ref.dtype)
        count = jnp.zeros(ids.shape, ids.dtype)
        one = jnp.ones(ids.shape, ids.dtype)
        for k in range(wide_ref.shape[0]):
            count = count + jnp.where(wide_ref[k] == ids, one, jnp.zeros_like(one))
        x_ref[t ^ plan_ref[0]] = (count.astype(F32) * scale).astype(x_ref.dtype)
        return carry

    lax.fori_loop(0, x_ref.shape[0], body, 0, unroll=4)
    for i, copy in enumerate(copies):
        copy.wait()
        multiply_tiles(
            src_ref, dst_ref, None, x_ref, held_ref, acc_ref, i * STREAM, STREAM, 0, tiles
        )
    store_chunks(acc_ref, out_refs, orders, 1.0)


def first_pass(src, dst, plan, seed_t, w, n_src, orders, scale):
    seeds = seed_t.shape[1]
    sizes = [len(order) for order in orders]
    return pl.pallas_call(
        functools.partial(first_kernel, orders=orders, scale=scale),
        in_specs=[SMEM] * 3 + [VMEM, pl.BlockSpec(memory_space=pltpu.HBM)],
        out_specs=[VMEM] * (1 + len(sizes)),
        scratch_shapes=[
            pltpu.VMEM((n_src, seeds, EDGE), BF16),
            pltpu.VMEM((seed_t.shape[0], seeds, EDGE), jnp.int16),
            pltpu.VMEM((sum(sizes), seeds, EDGE), F32),
            pltpu.SemaphoreType.DMA((w.shape[0] // STREAM,)),
        ],
        out_shape=[pltpu.VMEM((2 * w.shape[0], EDGE, EDGE), w.dtype)]
        + [jax.ShapeDtypeStruct((rows, seeds, EDGE), BF16) for rows in sizes],
        compiler_params=pltpu.CompilerParams(vmem_limit_bytes=37 * MIB),
        cost_estimate=LIGHT,
    )(src, dst, plan, seed_t, w)


def pass_kernel(src_ref, dst_ref, w_ref, *rest, flipped, in_orders, out_orders, wire):
    n_in = len(in_orders)
    in_refs, (*out_refs, x_ref, acc_ref) = rest[:n_in], rest[n_in:]
    acc_ref[...] = jnp.zeros_like(acc_ref)
    for ref, order in zip(in_refs, in_orders):
        for i, tile in enumerate(order):
            x_ref[tile] = ref[i]

    masks = None
    tiles = w_ref.shape[0] // 2
    base = tiles if flipped else 0

    def body(i, carry):
        multiply_tiles(src_ref, dst_ref, masks, x_ref, w_ref, acc_ref, i * UNROLL, UNROLL, base)
        return carry

    lax.fori_loop(0, tiles // UNROLL, body, 0)
    if not wire:
        store_chunks(acc_ref, out_refs, out_orders, SHRINK)
        return
    store_chunks(acc_ref, out_refs[:1], out_orders[:1], SHRINK)
    for out, order in zip(out_refs[1:], out_orders[1:]):
        top = acc_ref[order[0]]
        for tile in order[1:]:
            top = jnp.maximum(top, acc_ref[tile])
        top = jnp.max(top, axis=1, keepdims=True) * SHRINK
        power = jnp.ceil(jnp.log2(jnp.maximum(top, 1e-30))) - 14.0
        factor = jnp.exp2(-power) * SHRINK
        for i, tile in enumerate(order):
            out[i] = (acc_ref[tile] * factor).astype(out.dtype)
        out[len(order)] = jnp.broadcast_to(power, out.shape[1:]).astype(out.dtype)


def tile_pass(src, dst, held, flipped, parts, in_orders, out_orders, dtype, wire=None):
    seeds = parts[0].shape[1]
    sizes = [len(order) for order in out_orders]
    out_shape = [jax.ShapeDtypeStruct((rows, seeds, EDGE), dtype) for rows in sizes]
    if wire is not None:
        out_shape[1:] = [jax.ShapeDtypeStruct((rows + 1, seeds, EDGE), wire) for rows in sizes[1:]]
    return pl.pallas_call(
        functools.partial(
            pass_kernel, flipped=flipped, in_orders=in_orders, out_orders=out_orders, wire=wire is not None
        ),
        in_specs=[SMEM] * 2 + [VMEM] * (1 + len(parts)),
        out_specs=[VMEM] * len(sizes),
        scratch_shapes=[
            pltpu.VMEM((sum(p.shape[0] for p in parts), seeds, EDGE), BF16),
            pltpu.VMEM((sum(sizes), seeds, EDGE), F32),
        ],
        out_shape=out_shape,
        compiler_params=pltpu.CompilerParams(vmem_limit_bytes=16 * MIB),
        cost_estimate=LIGHT,
    )(src, dst, held, *parts)


def diag_mask(seeds, width, slot):
    lane = lax.broadcasted_iota(jnp.int32, (seeds, width), 1)
    sub = lax.broadcasted_iota(jnp.int32, (seeds, width), 0)
    return lane == sub + slot * seeds


def stat_kernel(x1_ref, y2_ref, *rest):
    *got_refs, w2_ref, stat_ref = rest
    seeds = w2_ref.shape[1]
    w2_ref[...] = added([ref[...] for ref in got_refs])

    def dot(a, b):
        return jnp.sum(jnp.sum(a * b, axis=0), axis=1, keepdims=True)

    x1, y2, w2 = x1_ref[...], y2_ref[...], w2_ref[...]
    spread = jnp.zeros((seeds, EDGE), F32)
    for slot, value in enumerate((dot(x1, x1), dot(x1, y2), dot(y2, y2), dot(w2, w2))):
        spread = jnp.where(diag_mask(seeds, EDGE, slot), value, spread)
    stat_ref[...] = jnp.broadcast_to(jnp.sum(spread, axis=0, keepdims=True), stat_ref.shape)


def finish_kernel(
    base_ref, seed_ref, stat_ref, x1_ref, u1_ref, y2_ref, w2_ref, hub_ref, auth_ref, *, users, items, scale
):
    seeds = seed_ref.shape[1]
    total = jnp.sum(stat_ref[...], axis=0, keepdims=True)

    def stat(slot):
        return jnp.sum(jnp.where(diag_mask(seeds, EDGE, slot), total, 0.0), axis=1, keepdims=True)

    x1_sq, x1_y2, y2_sq, w2_sq = stat(0), stat(1), stat(2), stat(3)
    s_item1 = lax.rsqrt(x1_sq / items + 1e-06)
    gain = s_item1 * GROW
    s_user1 = lax.rsqrt(gain * gain * x1_y2 / users + 1e-06)
    alpha = 0.85 * s_item1 * s_user1 * (GROW * GROW)
    x2_sq = alpha * alpha * y2_sq + 0.3 * alpha * x1_y2 + 0.0225 * x1_sq
    s_item2 = lax.rsqrt(x2_sq / items + 1e-06)
    for t in range(auth_ref.shape[1] // EDGE):
        auth_ref[:, t * EDGE : (t + 1) * EDGE] = (alpha * y2_ref[t] + 0.15 * x1_ref[t]) * s_item2
    raw_sq = alpha * alpha * w2_sq + 0.3 * alpha * y2_sq + 0.0225 * x1_y2
    out_gain = s_item2 * GROW
    s_user2 = lax.rsqrt(out_gain * out_gain * raw_sq / users + 1e-06)
    columns = seed_columns(seed_ref)
    for t in range(hub_ref.shape[1] // EDGE):
        raw = (alpha * w2_ref[t] + 0.15 * u1_ref[t]) * out_gain
        tele = teleport_tile(columns, base_ref[0] + t * EDGE, scale)
        hub_ref[:, t * EDGE : (t + 1) * EDGE] = 0.85 * raw * s_user2 + 0.15 * tele


def per_device(tile_values, tile_rows, tile_cols, seed_users):
    n_rows = lax.axis_size("row")
    n_cols = lax.axis_size("col")
    row = lax.axis_index("row").astype(jnp.int32)
    col = lax.axis_index("col").astype(jnp.int32)
    seeds = seed_users.shape[0]
    users = U_DEV * n_rows * n_cols
    items = I_DEV * n_rows * n_cols
    scale = float(np.float32((users / SEEDK) ** 0.5))
    seed_t = seed_users.T
    core, y, zhi = field(row, CORE), field(row, Y), field(row, ZHI)
    zlo, x = field(col, ZLO), field(col, X)
    own_base = ((row * n_cols + col) * U_DEV).reshape(1)
    zero = jnp.zeros((), jnp.int32)
    item_core, item_core_y = core << 1, (core << 1) | (y << 2)
    user_x, user_x_z = x << 4, (x << 4) | (zlo << 2)
    plan = jnp.stack([user_x, zero, row * (U_DEV * n_cols)])
    cols1, cols2 = tile_cols ^ item_core, tile_cols ^ item_core_y
    rows1, rows2 = tile_rows ^ user_x, tile_rows ^ user_x_z
    held, keep, send = first_pass(
        rows1, cols1, plan, seed_t, tile_values, 64, HALVES_ZY, scale
    )
    (part,) = add_parts(held, exchanged([keep, send], "row", CORE), [BF16])
    (part,) = add_parts(held, gathered(part, "row", ZHI), [BF16])
    x1_all, part = add_parts(held, gathered(part, "row", Y), [F32, BF16])
    x1 = lax.dynamic_slice_in_dim(x1_all, (zhi * 4 + y) * 2, 2, 0)

    chunks = tile_pass(
        cols1, rows1, held, True, gathered(part, "row", CORE), HALVES_ZY, QUARTERS, BF16
    )
    (part,) = add_parts(held, exchanged(chunks, "col", X), [BF16])
    (part,) = add_parts(held, gathered(part, "col", (1, 1)), [BF16])
    u1_all, part = add_parts(held, gathered(part, "col", (0, 1)), [F32, BF16])
    u1 = lax.dynamic_slice_in_dim(u1_all, zlo * 4, 4, 0)

    chunks = tile_pass(
        rows1, cols2, held, False, gathered(part, "col", X), QUARTERS, HALVES_YZ, F32
    )
    (part,) = add_parts(held, exchanged(chunks, "row", CORE), [F32])
    (part,) = add_parts(held, exchanged([part[i * 4 : i * 4 + 4] for i in range(4)], "row", Y), [F32])
    y2_all, part = add_parts(held, gathered(part, "row", ZHI), [F32, BF16])
    y2 = lax.dynamic_slice_in_dim(y2_all, zhi * 2, 2, 0)
    half = jnp.concatenate(gathered(part, "row", Y), axis=0)

    own, *others = tile_pass(
        cols2, rows2, held, True, gathered(half, "row", CORE), HALVES_YZ, QUARTERS, F32, WIRE
    )
    part = add_scaled(own, exchanged([own] + [o.astype(F16) for o in others], "col", X)[1:])
    got = exchanged([part[i * 4 : i * 4 + 4] for i in range(4)], "col", ZLO)
    small = pltpu.CompilerParams(vmem_limit_bytes=8 * MIB)
    w2, stat = pl.pallas_call(
        stat_kernel,
        in_specs=[VMEM] * (2 + len(got)),
        out_specs=[VMEM] * 2,
        out_shape=[
            jax.ShapeDtypeStruct((U_DEV // EDGE, seeds, EDGE), F32),
            jax.ShapeDtypeStruct((n_rows * n_cols, EDGE), F32),
        ],
        compiler_params=small,
    )(x1, y2, *got)
    stats = lax.all_to_all(stat.reshape(n_rows * n_cols, 1, EDGE), ("row", "col"), 0, 0)
    return pl.pallas_call(
        functools.partial(finish_kernel, users=users, items=items, scale=scale),
        in_specs=[SMEM] + [VMEM] * 6,
        out_specs=[VMEM] * 2,
        out_shape=[
            jax.ShapeDtypeStruct((seeds, U_DEV), F32),
            jax.ShapeDtypeStruct((seeds, I_DEV), F32),
        ],
        compiler_params=small,
    )(own_base, seed_t, stats.reshape(n_rows * n_cols, EDGE), x1, u1, y2, w2)


def solution(mesh):
    return jax.shard_map(
        per_device,
        mesh=mesh,
        in_specs=(P(("row", "col"), None, None), P(("row", "col")), P(("row", "col")), P()),
        out_specs=(P(None, ("row", "col")), P(None, ("col", "row"))),
        check_vma=False,
    )
```

```python
import functools
import jax
import jax.numpy as jnp
import numpy as np
from jax import lax
from jax.experimental import pallas as pl
from jax.experimental.pallas import tpu as pltpu
from jax.sharding import PartitionSpec as P

SEEDK = 16
U_DEV = 512
I_DEV = 256
EDGE = 128
UNROLL = 176
STREAM = 88
SHRINK = 2.0**-16
GROW = 2.0**16
MIB = 2**20
LIGHT = pl.CostEstimate(flops=10**6, bytes_accessed=10**5, transcendentals=0)
F32 = jnp.float32
BF16 = jnp.bfloat16
F16 = jnp.float16
WIRE = F32
SMEM = pl.BlockSpec(memory_space=pltpu.SMEM)
VMEM = pl.BlockSpec(memory_space=pltpu.VMEM)

CORE, Y, ZHI = (0, 1), (1, 2), (3, 1)
ZLO, X = (0, 2), (2, 2)


HALVES_ZY = [[z * 16 + y * 4 + h * 2 + q for z in range(2) for y in range(4) for q in range(2)] for h in range(2)]
HALVES_YZ = [[z * 16 + y * 4 + h * 2 + q for y in range(4) for z in range(2) for q in range(2)] for h in range(2)]
QUARTERS = [list(range(c * 16, c * 16 + 16)) for c in range(4)]


def field(index, part):
    return (index >> part[0]) & ((1 << part[1]) - 1)


def swapped(x, axis, part, by):
    return lax.ppermute(x, axis, [(i, i ^ (by << part[0])) for i in range(16)])


def gathered(x, axis, part):
    return [x] + [swapped(x, axis, part, by) for by in range(1, 1 << part[1])]


def exchanged(chunks, axis, part):
    return [chunks[0]] + [swapped(c, axis, part, by) for by, c in enumerate(chunks) if by]


def added(parts):
    total = parts[0].astype(F32)
    for p in parts[1:]:
        total = total + p.astype(F32)
    return total


def add_kernel(*refs, n_in):
    total = added([ref[...] for ref in refs[1 : 1 + n_in]])
    for out in refs[1 + n_in :]:
        out[...] = total.astype(out.dtype)


def add_parts(held, parts, dtypes):
    return pl.pallas_call(
        functools.partial(add_kernel, n_in=len(parts)),
        in_specs=[VMEM] * (1 + len(parts)),
        out_specs=[VMEM] * len(dtypes),
        out_shape=[jax.ShapeDtypeStruct(parts[0].shape, dtype) for dtype in dtypes],
        compiler_params=pltpu.CompilerParams(vmem_limit_bytes=8 * MIB),
        cost_estimate=LIGHT,
    )(held, *parts)


def add_scaled(own, others):
    total = own
    for other in others:
        wide = other.astype(F32)
        total = total + wide[:-1] * jnp.exp2(wide[-1:])
    return total


def seed_columns(seed_ref):
    k, seeds = seed_ref.shape
    diag = diag_mask(seeds, seeds, 0)
    rows = seed_ref[...].astype(F32)
    return [
        jnp.sum(jnp.where(diag, rows[i : i + 1], 0.0), axis=1, keepdims=True).astype(jnp.int32)
        for i in range(k)
    ]


def teleport_tile(columns, base, scale):
    seeds = columns[0].shape[0]
    ids = base + lax.broadcasted_iota(jnp.int32, (seeds, EDGE), 1)
    count = jnp.zeros((seeds, EDGE), F32)
    for column in columns:
        count = jnp.where(column == ids, count + 1.0, count)
    return count * scale


def multiply_tiles(src_ref, dst_ref, x_ref, w_ref, acc_ref, first, count, base, mask=0, flip=0):
    for j in range(count):
        tile = w_ref[base + first + j]
        prod = lax.dot_general(
            x_ref[src_ref[first + j]],
            tile,
            (((1,), (0,)), ((), ())),
            preferred_element_type=F32,
        )
        acc_ref[dst_ref[first + j] ^ mask] += prod
        if flip:
            w_ref[flip + first + j] = tile.T


def store_chunks(acc_ref, out_refs, orders, factor):
    for out, order in zip(out_refs, orders):
        for i, tile in enumerate(order):
            out[i] = (acc_ref[tile] * factor).astype(out.dtype)


def first_kernel(src_ref, dst_ref, seed_ref, w_ref, held_ref, *rest, orders, scale):
    *out_refs, x_ref, wide_ref, acc_ref, sem = rest
    copies = []
    tiles = w_ref.shape[0]
    for i in range(tiles // STREAM):
        part = pl.ds(i * STREAM, STREAM)
        copies.append(pltpu.make_async_copy(w_ref.at[part], held_ref.at[part], sem.at[i]))
        copies[-1].start()
    acc_ref[...] = jnp.zeros_like(acc_ref)
    row = lax.axis_index("row")
    mask = field(row, CORE) << 1
    last = x_ref.shape[0] * EDGE
    for k, column in enumerate(seed_columns(seed_ref)):
        local = column - row * last
        local = jnp.where((local >= 0) & (local < last), local, -1)
        wide_ref[k] = jnp.broadcast_to(local, wide_ref.shape[1:]).astype(wide_ref.dtype)

    lanes = lax.broadcasted_iota(jnp.int32, wide_ref.shape[1:], 1)

    def body(t, carry):
        ids = (t * EDGE + lanes).astype(wide_ref.dtype)
        count = jnp.zeros(ids.shape, ids.dtype)
        one = jnp.ones(ids.shape, ids.dtype)
        for k in range(wide_ref.shape[0]):
            count = count + jnp.where(wide_ref[k] == ids, one, jnp.zeros_like(one))
        x_ref[t] = (count.astype(F32) * scale).astype(x_ref.dtype)
        return carry

    lax.fori_loop(0, x_ref.shape[0], body, 0, unroll=4)
    for i, copy in enumerate(copies):
        copy.wait()
        multiply_tiles(
            src_ref, dst_ref, x_ref, held_ref, acc_ref, i * STREAM, STREAM, 0, mask, tiles
        )
    store_chunks(acc_ref, out_refs, orders, 1.0)


def first_pass(src, dst, seed_t, w, n_src, orders, scale):
    seeds = seed_t.shape[1]
    sizes = [len(order) for order in orders]
    return pl.pallas_call(
        functools.partial(first_kernel, orders=orders, scale=scale),
        in_specs=[SMEM] * 2 + [VMEM, pl.BlockSpec(memory_space=pltpu.HBM)],
        out_specs=[VMEM] * (1 + len(sizes)),
        scratch_shapes=[
            pltpu.VMEM((n_src, seeds, EDGE), BF16),
            pltpu.VMEM((seed_t.shape[0], seeds, EDGE), jnp.int16),
            pltpu.VMEM((sum(sizes), seeds, EDGE), F32),
            pltpu.SemaphoreType.DMA((w.shape[0] // STREAM,)),
        ],
        out_shape=[pltpu.VMEM((2 * w.shape[0], EDGE, EDGE), w.dtype)]
        + [jax.ShapeDtypeStruct((rows, seeds, EDGE), BF16) for rows in sizes],
        compiler_params=pltpu.CompilerParams(vmem_limit_bytes=33 * MIB),
        cost_estimate=LIGHT,
    )(src, dst, seed_t, w)


def pass_kernel(src_ref, dst_ref, w_ref, *rest, flipped, in_orders, out_orders, wire):
    n_in = len(in_orders)
    in_refs, (*out_refs, x_ref, acc_ref) = rest[:n_in], rest[n_in:]
    acc_ref[...] = jnp.zeros_like(acc_ref)
    for ref, order in zip(in_refs, in_orders):
        for i, tile in enumerate(order):
            x_ref[tile] = ref[i]

    tiles = w_ref.shape[0] // 2
    base = tiles if flipped else 0

    def body(i, carry):
        multiply_tiles(src_ref, dst_ref, x_ref, w_ref, acc_ref, i * UNROLL, UNROLL, base)
        return carry

    lax.fori_loop(0, tiles // UNROLL, body, 0)
    if not wire:
        store_chunks(acc_ref, out_refs, out_orders, SHRINK)
        return
    store_chunks(acc_ref, out_refs[:1], out_orders[:1], SHRINK)
    for out, order in zip(out_refs[1:], out_orders[1:]):
        top = acc_ref[order[0]]
        for tile in order[1:]:
            top = jnp.maximum(top, acc_ref[tile])
        top = jnp.max(top, axis=1, keepdims=True) * SHRINK
        power = jnp.ceil(jnp.log2(jnp.maximum(top, 1e-30))) - 14.0
        factor = jnp.exp2(-power) * SHRINK
        for i, tile in enumerate(order):
            out[i] = (acc_ref[tile] * factor).astype(out.dtype)
        out[len(order)] = jnp.broadcast_to(power, out.shape[1:]).astype(out.dtype)


def tile_pass(src, dst, held, flipped, parts, in_orders, out_orders, dtype, wire=None):
    seeds = parts[0].shape[1]
    sizes = [len(order) for order in out_orders]
    out_shape = [jax.ShapeDtypeStruct((rows, seeds, EDGE), dtype) for rows in sizes]
    if wire is not None:
        out_shape[1:] = [jax.ShapeDtypeStruct((rows + 1, seeds, EDGE), wire) for rows in sizes[1:]]
    return pl.pallas_call(
        functools.partial(
            pass_kernel, flipped=flipped, in_orders=in_orders, out_orders=out_orders, wire=wire is not None
        ),
        in_specs=[SMEM] * 2 + [VMEM] * (1 + len(parts)),
        out_specs=[VMEM] * len(sizes),
        scratch_shapes=[
            pltpu.VMEM((sum(p.shape[0] for p in parts), seeds, EDGE), BF16),
            pltpu.VMEM((sum(sizes), seeds, EDGE), F32),
        ],
        out_shape=out_shape,
        compiler_params=pltpu.CompilerParams(vmem_limit_bytes=16 * MIB),
        cost_estimate=LIGHT,
    )(src, dst, held, *parts)


def diag_mask(seeds, width, slot):
    lane = lax.broadcasted_iota(jnp.int32, (seeds, width), 1)
    sub = lax.broadcasted_iota(jnp.int32, (seeds, width), 0)
    return lane == sub + slot * seeds


def stat_kernel(x1_ref, y2_ref, *rest):
    *got_refs, w2_ref, stat_ref = rest
    seeds = w2_ref.shape[1]
    w2_ref[...] = added([ref[...] for ref in got_refs])

    def dot(a, b):
        return jnp.sum(jnp.sum(a * b, axis=0), axis=1, keepdims=True)

    x1, y2, w2 = x1_ref[...], y2_ref[...], w2_ref[...]
    spread = jnp.zeros((seeds, EDGE), F32)
    for slot, value in enumerate((dot(x1, x1), dot(x1, y2), dot(y2, y2), dot(w2, w2))):
        spread = jnp.where(diag_mask(seeds, EDGE, slot), value, spread)
    stat_ref[...] = jnp.broadcast_to(jnp.sum(spread, axis=0, keepdims=True), stat_ref.shape)


def finish_kernel(
    seed_ref, stat_ref, x1_ref, u1_ref, y2_ref, w2_ref, hub_ref, auth_ref, *, users, items, scale
):
    seeds = seed_ref.shape[1]
    total = jnp.sum(stat_ref[...], axis=0, keepdims=True)

    def stat(slot):
        return jnp.sum(jnp.where(diag_mask(seeds, EDGE, slot), total, 0.0), axis=1, keepdims=True)

    x1_sq, x1_y2, y2_sq, w2_sq = stat(0), stat(1), stat(2), stat(3)
    s_item1 = lax.rsqrt(x1_sq / items + 1e-06)
    gain = s_item1 * GROW
    s_user1 = lax.rsqrt(gain * gain * x1_y2 / users + 1e-06)
    alpha = 0.85 * s_item1 * s_user1 * (GROW * GROW)
    x2_sq = alpha * alpha * y2_sq + 0.3 * alpha * x1_y2 + 0.0225 * x1_sq
    s_item2 = lax.rsqrt(x2_sq / items + 1e-06)
    for t in range(auth_ref.shape[1] // EDGE):
        auth_ref[:, t * EDGE : (t + 1) * EDGE] = (alpha * y2_ref[t] + 0.15 * x1_ref[t]) * s_item2
    raw_sq = alpha * alpha * w2_sq + 0.3 * alpha * y2_sq + 0.0225 * x1_y2
    out_gain = s_item2 * GROW
    s_user2 = lax.rsqrt(out_gain * out_gain * raw_sq / users + 1e-06)
    columns = seed_columns(seed_ref)
    base = (lax.axis_index("row") * lax.axis_size("col") + lax.axis_index("col")) * hub_ref.shape[1]
    for t in range(hub_ref.shape[1] // EDGE):
        raw = (alpha * w2_ref[t] + 0.15 * u1_ref[t]) * out_gain
        tele = teleport_tile(columns, base + t * EDGE, scale)
        hub_ref[:, t * EDGE : (t + 1) * EDGE] = 0.85 * raw * s_user2 + 0.15 * tele


def per_device(tile_values, tile_rows, tile_cols, seed_users):
    n_rows = lax.axis_size("row")
    n_cols = lax.axis_size("col")
    row = lax.axis_index("row").astype(jnp.int32)
    col = lax.axis_index("col").astype(jnp.int32)
    seeds = seed_users.shape[0]
    users = U_DEV * n_rows * n_cols
    items = I_DEV * n_rows * n_cols
    scale = float(np.float32((users / SEEDK) ** 0.5))
    seed_t = seed_users.T
    core, y, zhi = field(row, CORE), field(row, Y), field(row, ZHI)
    zlo, x = field(col, ZLO), field(col, X)
    item_core, item_core_y = core << 1, (core << 1) | (y << 2)
    user_x, user_x_z = x << 4, (x << 4) | (zlo << 2)
    cols1, cols2 = tile_cols ^ item_core, tile_cols ^ item_core_y
    rows1, rows2 = tile_rows ^ user_x, tile_rows ^ user_x_z
    held, keep, send = first_pass(
        tile_rows, tile_cols, seed_t, tile_values, 64, HALVES_ZY, scale
    )
    keep, send, rows1, cols1, rows2, cols2 = lax.optimization_barrier((keep, send, rows1, cols1, rows2, cols2))
    (part,) = add_parts(held, exchanged([keep, send], "row", CORE), [BF16])
    (part,) = add_parts(held, gathered(part, "row", ZHI), [BF16])
    x1_all, part = add_parts(held, gathered(part, "row", Y), [F32, BF16])
    x1 = lax.dynamic_slice_in_dim(x1_all, (zhi * 4 + y) * 2, 2, 0)

    chunks = tile_pass(
        cols1, rows1, held, True, gathered(part, "row", CORE), HALVES_ZY, QUARTERS, BF16
    )
    (part,) = add_parts(held, exchanged(chunks, "col", X), [BF16])
    (part,) = add_parts(held, gathered(part, "col", (1, 1)), [BF16])
    u1_all, part = add_parts(held, gathered(part, "col", (0, 1)), [F32, BF16])
    u1 = lax.dynamic_slice_in_dim(u1_all, zlo * 4, 4, 0)

    chunks = tile_pass(
        rows1, cols2, held, False, gathered(part, "col", X), QUARTERS, HALVES_YZ, F32
    )
    (part,) = add_parts(held, exchanged(chunks, "row", CORE), [F32])
    (part,) = add_parts(held, exchanged([part[i * 4 : i * 4 + 4] for i in range(4)], "row", Y), [F32])
    y2_all, part = add_parts(held, gathered(part, "row", ZHI), [F32, BF16])
    y2 = lax.dynamic_slice_in_dim(y2_all, zhi * 2, 2, 0)
    half = jnp.concatenate(gathered(part, "row", Y), axis=0)

    own, *others = tile_pass(
        cols2, rows2, held, True, gathered(half, "row", CORE), HALVES_YZ, QUARTERS, F32, WIRE
    )
    part = add_scaled(own, exchanged([own] + [o.astype(F16) for o in others], "col", X)[1:])
    got = exchanged([part[i * 4 : i * 4 + 4] for i in range(4)], "col", ZLO)
    small = pltpu.CompilerParams(vmem_limit_bytes=8 * MIB)
    w2, stat = pl.pallas_call(
        stat_kernel,
        in_specs=[VMEM] * (2 + len(got)),
        out_specs=[VMEM] * 2,
        out_shape=[
            jax.ShapeDtypeStruct((U_DEV // EDGE, seeds, EDGE), F32),
            jax.ShapeDtypeStruct((n_rows * n_cols, EDGE), F32),
        ],
        compiler_params=small,
    )(x1, y2, *got)
    stats = lax.all_to_all(stat.reshape(n_rows * n_cols, 1, EDGE), ("row", "col"), 0, 0)
    return pl.pallas_call(
        functools.partial(finish_kernel, users=users, items=items, scale=scale),
        in_specs=[VMEM] * 6,
        out_specs=[VMEM] * 2,
        out_shape=[
            jax.ShapeDtypeStruct((seeds, U_DEV), F32),
            jax.ShapeDtypeStruct((seeds, I_DEV), F32),
        ],
        compiler_params=small,
    )(seed_t, stats.reshape(n_rows * n_cols, EDGE), x1, u1, y2, w2)


def solution(mesh):
    return jax.shard_map(
        per_device,
        mesh=mesh,
        in_specs=(P(("row", "col"), None, None), P(("row", "col")), P(("row", "col")), P()),
        out_specs=(P(None, ("row", "col")), P(None, ("col", "row"))),
        check_vma=False,
    )
```

```python
import functools
import jax
import jax.numpy as jnp
import numpy as np
from jax import lax
from jax.experimental import pallas as pl
from jax.experimental.pallas import tpu as pltpu
from jax.sharding import PartitionSpec as P

SEEDK = 16
U_DEV = 512
I_DEV = 256
EDGE = 128
UNROLL = 176
STREAM = 88
SHRINK = 2.0**-16
GROW = 2.0**16
MIB = 2**20
LIGHT = pl.CostEstimate(flops=10**6, bytes_accessed=10**5, transcendentals=0)
F32 = jnp.float32
BF16 = jnp.bfloat16
F16 = jnp.float16
WIRE = F32
SMEM = pl.BlockSpec(memory_space=pltpu.SMEM)
VMEM = pl.BlockSpec(memory_space=pltpu.VMEM)

CORE, Y, ZHI = (0, 1), (1, 2), (3, 1)
ZLO, X = (0, 2), (2, 2)


HALVES_ZY = [[z * 16 + y * 4 + h * 2 + q for z in range(2) for y in range(4) for q in range(2)] for h in range(2)]
HALVES_YZ = [[z * 16 + y * 4 + h * 2 + q for y in range(4) for z in range(2) for q in range(2)] for h in range(2)]
QUARTERS = [list(range(c * 16, c * 16 + 16)) for c in range(4)]


def field(index, part):
    return (index >> part[0]) & ((1 << part[1]) - 1)


def swapped(x, axis, part, by):
    return lax.ppermute(x, axis, [(i, i ^ (by << part[0])) for i in range(16)])


def gathered(x, axis, part):
    return [x] + [swapped(x, axis, part, by) for by in range(1, 1 << part[1])]


def exchanged(chunks, axis, part):
    return [chunks[0]] + [swapped(c, axis, part, by) for by, c in enumerate(chunks) if by]


def added(parts):
    total = parts[0].astype(F32)
    for p in parts[1:]:
        total = total + p.astype(F32)
    return total


def add_kernel(*refs, n_in):
    total = added([ref[...] for ref in refs[1 : 1 + n_in]])
    for out in refs[1 + n_in :]:
        out[...] = total.astype(out.dtype)


def add_parts(held, parts, dtypes):
    return pl.pallas_call(
        functools.partial(add_kernel, n_in=len(parts)),
        in_specs=[VMEM] * (1 + len(parts)),
        out_specs=[VMEM] * len(dtypes),
        out_shape=[jax.ShapeDtypeStruct(parts[0].shape, dtype) for dtype in dtypes],
        compiler_params=pltpu.CompilerParams(vmem_limit_bytes=8 * MIB),
        cost_estimate=LIGHT,
    )(held, *parts)


def add_scaled(own, others):
    total = own
    for other in others:
        wide = other.astype(F32)
        total = total + wide[:-1] * jnp.exp2(wide[-1:])
    return total


def seed_columns(seed_ref):
    k, seeds = seed_ref.shape
    diag = diag_mask(seeds, seeds, 0)
    rows = seed_ref[...].astype(F32)
    return [
        jnp.sum(jnp.where(diag, rows[i : i + 1], 0.0), axis=1, keepdims=True).astype(jnp.int32)
        for i in range(k)
    ]


def teleport_tile(columns, base, scale):
    seeds = columns[0].shape[0]
    ids = base + lax.broadcasted_iota(jnp.int32, (seeds, EDGE), 1)
    count = jnp.zeros((seeds, EDGE), F32)
    for column in columns:
        count = jnp.where(column == ids, count + 1.0, count)
    return count * scale


def multiply_tiles(src_ref, dst_ref, x_ref, w_ref, acc_ref, first, count, base, mask=0, flip=0):
    for j in range(count):
        tile = w_ref[base + first + j]
        prod = lax.dot_general(
            x_ref[src_ref[first + j]],
            tile,
            (((1,), (0,)), ((), ())),
            preferred_element_type=F32,
        )
        acc_ref[dst_ref[first + j] ^ mask] += prod
        if flip:
            w_ref[flip + first + j] = tile.T


def store_chunks(acc_ref, out_refs, orders, factor):
    for out, order in zip(out_refs, orders):
        for i, tile in enumerate(order):
            out[i] = (acc_ref[tile] * factor).astype(out.dtype)


def first_kernel(src_ref, dst_ref, seed_ref, w_ref, held_ref, *rest, orders, scale):
    *out_refs, x_ref, wide_ref, acc_ref, sem = rest
    copies = []
    tiles = w_ref.shape[0]
    for i in range(tiles // STREAM):
        part = pl.ds(i * STREAM, STREAM)
        copies.append(pltpu.make_async_copy(w_ref.at[part], held_ref.at[part], sem.at[i]))
        copies[-1].start()
    acc_ref[...] = jnp.zeros_like(acc_ref)
    row = lax.axis_index("row")
    mask = field(row, CORE) << 1
    last = x_ref.shape[0] * EDGE
    for k, column in enumerate(seed_columns(seed_ref)):
        local = column - row * last
        local = jnp.where((local >= 0) & (local < last), local, -1)
        wide_ref[k] = jnp.broadcast_to(local, wide_ref.shape[1:]).astype(wide_ref.dtype)

    lanes = lax.broadcasted_iota(jnp.int32, wide_ref.shape[1:], 1)

    def body(t, carry):
        ids = (t * EDGE + lanes).astype(wide_ref.dtype)
        count = jnp.zeros(ids.shape, ids.dtype)
        one = jnp.ones(ids.shape, ids.dtype)
        for k in range(wide_ref.shape[0]):
            count = count + jnp.where(wide_ref[k] == ids, one, jnp.zeros_like(one))
        x_ref[t] = (count.astype(F32) * scale).astype(x_ref.dtype)
        return carry

    lax.fori_loop(0, x_ref.shape[0], body, 0, unroll=4)
    for i, copy in enumerate(copies):
        copy.wait()
        multiply_tiles(
            src_ref, dst_ref, x_ref, held_ref, acc_ref, i * STREAM, STREAM, 0, mask, tiles
        )
    store_chunks(acc_ref, out_refs, orders, 1.0)


def first_pass(src, dst, seed_t, w, n_src, orders, scale):
    seeds = seed_t.shape[1]
    sizes = [len(order) for order in orders]
    return pl.pallas_call(
        functools.partial(first_kernel, orders=orders, scale=scale),
        in_specs=[SMEM] * 2 + [VMEM, pl.BlockSpec(memory_space=pltpu.HBM)],
        out_specs=[VMEM] * (1 + len(sizes)),
        scratch_shapes=[
            pltpu.VMEM((n_src, seeds, EDGE), BF16),
            pltpu.VMEM((seed_t.shape[0], seeds, EDGE), jnp.int16),
            pltpu.VMEM((sum(sizes), seeds, EDGE), F32),
            pltpu.SemaphoreType.DMA((w.shape[0] // STREAM,)),
        ],
        out_shape=[pltpu.VMEM((2 * w.shape[0], EDGE, EDGE), w.dtype)]
        + [jax.ShapeDtypeStruct((rows, seeds, EDGE), BF16) for rows in sizes],
        compiler_params=pltpu.CompilerParams(vmem_limit_bytes=33 * MIB),
        cost_estimate=LIGHT,
    )(src, dst, seed_t, w)


def pass_kernel(src_ref, dst_ref, w_ref, *rest, flipped, in_orders, out_orders, wire):
    n_in = len(in_orders)
    in_refs, (*out_refs, x_ref, acc_ref) = rest[:n_in], rest[n_in:]
    acc_ref[...] = jnp.zeros_like(acc_ref)
    for ref, order in zip(in_refs, in_orders):
        for i, tile in enumerate(order):
            x_ref[tile] = ref[i]

    tiles = w_ref.shape[0] // 2
    base = tiles if flipped else 0

    def body(i, carry):
        multiply_tiles(src_ref, dst_ref, x_ref, w_ref, acc_ref, i * UNROLL, UNROLL, base)
        return carry

    lax.fori_loop(0, tiles // UNROLL, body, 0)
    if not wire:
        store_chunks(acc_ref, out_refs, out_orders, SHRINK)
        return
    store_chunks(acc_ref, out_refs[:1], out_orders[:1], SHRINK)
    for out, order in zip(out_refs[1:], out_orders[1:]):
        top = acc_ref[order[0]]
        for tile in order[1:]:
            top = jnp.maximum(top, acc_ref[tile])
        top = jnp.max(top, axis=1, keepdims=True) * SHRINK
        power = jnp.ceil(jnp.log2(jnp.maximum(top, 1e-30))) - 14.0
        factor = jnp.exp2(-power) * SHRINK
        for i, tile in enumerate(order):
            out[i] = (acc_ref[tile] * factor).astype(out.dtype)
        out[len(order)] = jnp.broadcast_to(power, out.shape[1:]).astype(out.dtype)


def tile_pass(src, dst, held, flipped, parts, in_orders, out_orders, dtype, wire=None):
    seeds = parts[0].shape[1]
    sizes = [len(order) for order in out_orders]
    out_shape = [jax.ShapeDtypeStruct((rows, seeds, EDGE), dtype) for rows in sizes]
    if wire is not None:
        out_shape[1:] = [jax.ShapeDtypeStruct((rows + 1, seeds, EDGE), wire) for rows in sizes[1:]]
    return pl.pallas_call(
        functools.partial(
            pass_kernel, flipped=flipped, in_orders=in_orders, out_orders=out_orders, wire=wire is not None
        ),
        in_specs=[SMEM] * 2 + [VMEM] * (1 + len(parts)),
        out_specs=[VMEM] * len(sizes),
        scratch_shapes=[
            pltpu.VMEM((sum(p.shape[0] for p in parts), seeds, EDGE), BF16),
            pltpu.VMEM((sum(sizes), seeds, EDGE), F32),
        ],
        out_shape=out_shape,
        compiler_params=pltpu.CompilerParams(vmem_limit_bytes=16 * MIB),
        cost_estimate=LIGHT,
    )(src, dst, held, *parts)


def diag_mask(seeds, width, slot):
    lane = lax.broadcasted_iota(jnp.int32, (seeds, width), 1)
    sub = lax.broadcasted_iota(jnp.int32, (seeds, width), 0)
    return lane == sub + slot * seeds


def stat_kernel(x1_ref, y2_ref, *rest):
    *got_refs, w2_ref, stat_ref = rest
    seeds = w2_ref.shape[1]
    w2_ref[...] = added([ref[...] for ref in got_refs])

    def dot(a, b):
        return jnp.sum(jnp.sum(a * b, axis=0), axis=1, keepdims=True)

    x1, y2, w2 = x1_ref[...], y2_ref[...], w2_ref[...]
    spread = jnp.zeros((seeds, EDGE), F32)
    for slot, value in enumerate((dot(x1, x1), dot(x1, y2), dot(y2, y2), dot(w2, w2))):
        spread = jnp.where(diag_mask(seeds, EDGE, slot), value, spread)
    stat_ref[...] = jnp.broadcast_to(jnp.sum(spread, axis=0, keepdims=True), stat_ref.shape)


def finish_kernel(
    seed_ref, stat_ref, x1_ref, u1_ref, y2_ref, w2_ref, hub_ref, auth_ref, *, users, items, scale
):
    seeds = seed_ref.shape[1]
    total = jnp.sum(stat_ref[...], axis=0, keepdims=True)

    def stat(slot):
        return jnp.sum(jnp.where(diag_mask(seeds, EDGE, slot), total, 0.0), axis=1, keepdims=True)

    x1_sq, x1_y2, y2_sq, w2_sq = stat(0), stat(1), stat(2), stat(3)
    s_item1 = lax.rsqrt(x1_sq / items + 1e-06)
    gain = s_item1 * GROW
    s_user1 = lax.rsqrt(gain * gain * x1_y2 / users + 1e-06)
    alpha = 0.85 * s_item1 * s_user1 * (GROW * GROW)
    x2_sq = alpha * alpha * y2_sq + 0.3 * alpha * x1_y2 + 0.0225 * x1_sq
    s_item2 = lax.rsqrt(x2_sq / items + 1e-06)
    for t in range(auth_ref.shape[1] // EDGE):
        auth_ref[:, t * EDGE : (t + 1) * EDGE] = (alpha * y2_ref[t] + 0.15 * x1_ref[t]) * s_item2
    raw_sq = alpha * alpha * w2_sq + 0.3 * alpha * y2_sq + 0.0225 * x1_y2
    out_gain = s_item2 * GROW
    s_user2 = lax.rsqrt(out_gain * out_gain * raw_sq / users + 1e-06)
    columns = seed_columns(seed_ref)
    base = (lax.axis_index("row") * lax.axis_size("col") + lax.axis_index("col")) * hub_ref.shape[1]
    for t in range(hub_ref.shape[1] // EDGE):
        raw = (alpha * w2_ref[t] + 0.15 * u1_ref[t]) * out_gain
        tele = teleport_tile(columns, base + t * EDGE, scale)
        hub_ref[:, t * EDGE : (t + 1) * EDGE] = 0.85 * raw * s_user2 + 0.15 * tele


def per_device(tile_values, tile_rows, tile_cols, seed_users):
    n_rows = lax.axis_size("row")
    n_cols = lax.axis_size("col")
    row = lax.axis_index("row").astype(jnp.int32)
    col = lax.axis_index("col").astype(jnp.int32)
    seeds = seed_users.shape[0]
    users = U_DEV * n_rows * n_cols
    items = I_DEV * n_rows * n_cols
    scale = float(np.float32((users / SEEDK) ** 0.5))
    seed_t = seed_users.T
    core, y, zhi = field(row, CORE), field(row, Y), field(row, ZHI)
    zlo, x = field(col, ZLO), field(col, X)
    item_core, item_core_y = core << 1, (core << 1) | (y << 2)
    user_x, user_x_z = x << 4, (x << 4) | (zlo << 2)
    cols1, cols2 = tile_cols ^ item_core, tile_cols ^ item_core_y
    rows1, rows2 = tile_rows ^ user_x, tile_rows ^ user_x_z
    held, keep, send = first_pass(
        tile_rows, tile_cols, seed_t, tile_values, 64, HALVES_ZY, scale
    )
    keep, send, rows1, cols1, rows2, cols2 = lax.optimization_barrier((keep, send, rows1, cols1, rows2, cols2))
    part = added(exchanged([keep, send], "row", CORE)).astype(BF16)
    (part,) = add_parts(held, gathered(part, "row", ZHI), [BF16])
    x1_all, part = add_parts(held, gathered(part, "row", Y), [F32, BF16])
    x1 = lax.dynamic_slice_in_dim(x1_all, (zhi * 4 + y) * 2, 2, 0)

    chunks = tile_pass(
        cols1, rows1, held, True, gathered(part, "row", CORE), HALVES_ZY, QUARTERS, BF16
    )
    (part,) = add_parts(held, exchanged(chunks, "col", X), [BF16])
    (part,) = add_parts(held, gathered(part, "col", (1, 1)), [BF16])
    u1_all, part = add_parts(held, gathered(part, "col", (0, 1)), [F32, BF16])
    u1 = lax.dynamic_slice_in_dim(u1_all, zlo * 4, 4, 0)

    chunks = tile_pass(
        rows1, cols2, held, False, gathered(part, "col", X), QUARTERS, HALVES_YZ, F32
    )
    (part,) = add_parts(held, exchanged(chunks, "row", CORE), [F32])
    (part,) = add_parts(held, exchanged([part[i * 4 : i * 4 + 4] for i in range(4)], "row", Y), [F32])
    y2_all, part = add_parts(held, gathered(part, "row", ZHI), [F32, BF16])
    y2 = lax.dynamic_slice_in_dim(y2_all, zhi * 2, 2, 0)
    half = jnp.concatenate(gathered(part, "row", Y), axis=0)

    own, *others = tile_pass(
        cols2, rows2, held, True, gathered(half, "row", CORE), HALVES_YZ, QUARTERS, F32, WIRE
    )
    part = add_scaled(own, exchanged([own] + [o.astype(F16) for o in others], "col", X)[1:])
    got = exchanged([part[i * 4 : i * 4 + 4] for i in range(4)], "col", ZLO)
    small = pltpu.CompilerParams(vmem_limit_bytes=8 * MIB)
    w2, stat = pl.pallas_call(
        stat_kernel,
        in_specs=[VMEM] * (2 + len(got)),
        out_specs=[VMEM] * 2,
        out_shape=[
            jax.ShapeDtypeStruct((U_DEV // EDGE, seeds, EDGE), F32),
            jax.ShapeDtypeStruct((n_rows * n_cols, EDGE), F32),
        ],
        compiler_params=small,
    )(x1, y2, *got)
    stats = lax.all_to_all(stat.reshape(n_rows * n_cols, 1, EDGE), ("row", "col"), 0, 0)
    return pl.pallas_call(
        functools.partial(finish_kernel, users=users, items=items, scale=scale),
        in_specs=[VMEM] * 6,
        out_specs=[VMEM] * 2,
        out_shape=[
            jax.ShapeDtypeStruct((seeds, U_DEV), F32),
            jax.ShapeDtypeStruct((seeds, I_DEV), F32),
        ],
        compiler_params=small,
    )(seed_t, stats.reshape(n_rows * n_cols, EDGE), x1, u1, y2, w2)


def solution(mesh):
    return jax.shard_map(
        per_device,
        mesh=mesh,
        in_specs=(P(("row", "col"), None, None), P(("row", "col")), P(("row", "col")), P()),
        out_specs=(P(None, ("row", "col")), P(None, ("col", "row"))),
        check_vma=False,
    )
```
